32 devices in a mesh: seq: 8 (over y, x, core), head: 4 (over z).
Axes of the slice: x: 2, y: 2, z: 4, core: 2. Of those that a mesh axis runs over, the one named last changes fastest.
Arguments:
- head_inputs: bfloat16 [2, 4096, 8192], P(None, 'seq', 'head'), may hold values from -6 to 6
- gate_inputs: bfloat16 [2, 4096, 8192], P(None, 'seq', 'head'), may hold values from -6 to 6
- state_writes: bfloat16 [2, 4096, 1024], P(None, 'seq', 'head'), may hold values from -6 to 6
- state_reads: bfloat16 [2, 4096, 1024], P(None, 'seq', 'head'), may hold values from -6 to 6
- step_raw: float32 [2, 128, 4096], P(None, 'head', 'seq'), may hold values from -4 to 4
- decay_log: float32 [128], P('head')
- conv_inputs: float32 [4, 8192], P(None, 'head'), may hold values from -3 to 3
- conv_writes: float32 [4, 1024], P(None, 'head'), may hold values from -3 to 3
- conv_reads: float32 [4, 1024], P(None, 'head'), may hold values from -3 to 3
- norm_gain: float32 [8192], P('head'), may hold values from 0.1 to 1.9
- out_weight: bfloat16 [8192, 8192], P('head', 'seq'), may hold values from -0.0625 to 0.0625
Outputs:
- mixed: bfloat16 [2, 4096, 8192], P(None, 'seq', 'head')
The draws below stay inside these ranges and needn't reach their ends.
All inputs are finite; a program needn't handle non-finite values.
Results may differ from the reference program's by a relative error of at most 0.017.
Values may be sent and summed in bfloat16 or wider, within the bound.
A program may use at most 128 MiB of HBM per device.

```python
import math
import jax
import jax.numpy as jnp
from jax import lax

D_MODEL = 8192
HEADS = 128
HEAD_DIM = 64
STATE = 128
GROUPS = 8
CONV = 4
SPAN = 128
SEQS = 2
INNER = 8192
LEN = 4096
N_HEAD = 4


def draw_decay_log(key, part):
    key_kind, key_slow, key_fast = jax.random.split(jax.random.fold_in(key, 11), 3)
    slow = jax.random.randint(key_kind, (HEADS,), 0, 2).astype(jnp.float32)
    slow_rate = jax.random.uniform(key_slow, (HEADS,), jnp.float32, math.log(0.3), math.log(2.0)) - jnp.log(jnp.float32(LEN))
    fast_rate = jax.random.uniform(key_fast, (HEADS,), jnp.float32, math.log(1.0 / 50.0), math.log(1.0 / 20.0))
    return slow * slow_rate + (1.0 - slow) * fast_rate


def shard_levels(stream_key, extent, cuts, smallest, high):
    level = 1.0
    for dim, blocks in cuts:
        heights = jax.random.uniform(jax.random.fold_in(jax.random.fold_in(stream_key, 6), dim), (blocks,), jnp.float32, smallest / len(cuts), high / len(cuts))
        level = level * jnp.repeat(jnp.exp(heights), extent[dim] // blocks).reshape((-1,) + (1,) * (len(extent) - 1 - dim))
    return level


def normal_values(rng, dims, spread, bound, shards=(), held_as=jnp.bfloat16):
    factor_of = shard_levels(rng, dims, shards, -0.22, 0.18) if shards else 1.0
    drawn = jax.random.normal(rng, dims, jnp.float32) * spread * factor_of
    return jnp.minimum(jnp.maximum(drawn, -bound), bound).astype(held_as)


def setup_inputs(seed: int = 0) -> dict:
    key_list = jax.random.split(jax.random.key(seed), 12)
    return {
        "head_inputs": normal_values(key_list[0], (SEQS, LEN, INNER), 1.0, 6.0, ((1, 8), (2, 4))),
        "gate_inputs": normal_values(key_list[1], (SEQS, LEN, INNER), 1.0, 6.0, ((1, 8), (2, 4))),
        "state_writes": normal_values(key_list[2], (SEQS, LEN, GROUPS * STATE), 1.0, 6.0, ((1, 8), (2, 4))),
        "state_reads": normal_values(key_list[3], (SEQS, LEN, GROUPS * STATE), 1.0, 6.0, ((1, 8), (2, 4))),
        "step_raw": normal_values(key_list[4], (SEQS, HEADS, LEN), 1.0, 4.0, ((1, 4), (2, 8)), jnp.float32),
        "decay_log": draw_decay_log(jax.random.fold_in(key_list[11], 71), 0),
        "conv_inputs": normal_values(key_list[6], (CONV, INNER), CONV ** -0.5, 3.0, ((1, 4),), jnp.float32),
        "conv_writes": normal_values(key_list[7], (CONV, GROUPS * STATE), CONV ** -0.5, 3.0, ((1, 4),), jnp.float32),
        "conv_reads": normal_values(key_list[8], (CONV, GROUPS * STATE), CONV ** -0.5, 3.0, ((1, 4),), jnp.float32),
        "norm_gain": jnp.clip(1.0 + 0.18 * jax.random.normal(key_list[9], (INNER,), jnp.float32), 0.1, 1.9),
        "out_weight": normal_values(key_list[10], (INNER, D_MODEL), INNER ** -0.5, 0.0625, ((0, 4), (1, 8))),
    }


HIGH = lax.Precision.HIGHEST

def causal_conv(seq_in, weight):
    length = seq_in.shape[1]
    joined = jnp.pad(seq_in.astype(jnp.float32), ((0, 0), (CONV - 1, 0), (0, 0)))
    total = weight[0] * joined[:, 0:length]
    for tap in range(1, CONV):
        total = total + weight[tap] * joined[:, tap:tap + length]
    return jax.nn.silu(total)

def reference(head_inputs, gate_inputs, state_writes, state_reads, step_raw, decay_log, conv_inputs, conv_writes, conv_reads, norm_gain, out_weight):
    per_group = HEADS // GROUPS
    spans = LEN // SPAN
    group_width = INNER // GROUPS
    values = causal_conv(head_inputs, conv_inputs)
    writes = causal_conv(state_writes, conv_writes)
    reads = causal_conv(state_reads, conv_reads)
    steps = jax.nn.softplus(step_raw)
    log_decay = steps * (-jnp.exp(decay_log))[None, :, None]
    later = jnp.arange(SPAN)[:, None] >= jnp.arange(SPAN)[None, :]

    def one_span(state, block):
        vals, wrs, rds, stp, logs, gate = block
        cumul = jnp.cumsum(logs, axis=-1)
        scores = jnp.einsum('ign,jgn->gij', rds, wrs, precision=HIGH)
        gaps = jnp.where(later, cumul[:, :, None] - cumul[:, None, :], -jnp.inf)
        mixing = (jnp.exp(gaps) * stp[:, None, :]).reshape(GROUPS, per_group, SPAN, SPAN) * scores[:, None]
        vals_g = vals.reshape(SPAN, GROUPS, per_group, HEAD_DIM)
        diag = jnp.einsum('ghij,jghp->ighp', mixing, vals_g, precision=HIGH)
        state_g = state.reshape(GROUPS, per_group, STATE, HEAD_DIM)
        scale_in = jnp.exp(cumul).reshape(GROUPS, per_group, SPAN).transpose(2, 0, 1)
        reading = jnp.einsum('ign,ghnp->ighp', rds, state_g, precision=HIGH) * scale_in[..., None]
        ssd = (diag + reading).reshape(SPAN, INNER)
        gated = ssd * jax.nn.silu(gate.astype(jnp.float32))
        grouped = gated.reshape(SPAN, GROUPS, group_width)
        normed = grouped * lax.rsqrt(lax.optimization_barrier(jnp.mean(grouped * grouped, axis=-1, keepdims=True)) + 1e-05)
        normed = (normed.reshape(SPAN, INNER) * norm_gain).astype(jnp.bfloat16)
        weights_in = (jnp.exp(cumul[:, -1:] - cumul) * stp).reshape(GROUPS, per_group, SPAN)
        fresh = jnp.einsum('jgn,ghj,jghp->ghnp', wrs, weights_in, vals_g, precision=HIGH).reshape(HEADS, STATE, HEAD_DIM)
        new_state = jnp.exp(cumul[:, -1])[:, None, None] * state + fresh
        return (new_state, normed)
    outputs = []
    for seq_index in range(SEQS):
        blocks = (values[seq_index].reshape(spans, SPAN, HEADS, HEAD_DIM), writes[seq_index].reshape(spans, SPAN, GROUPS, STATE), reads[seq_index].reshape(spans, SPAN, GROUPS, STATE), steps[seq_index].reshape(HEADS, spans, SPAN).transpose(1, 0, 2), log_decay[seq_index].reshape(HEADS, spans, SPAN).transpose(1, 0, 2), gate_inputs[seq_index].reshape(spans, SPAN, INNER))
        start = jnp.zeros((HEADS, STATE, HEAD_DIM), jnp.float32)
        final_state, normed = lax.scan(one_span, start, blocks)
        outputs.append(normed.reshape(LEN, INNER))
    rows = jnp.stack(outputs, axis=0).reshape(SEQS * LEN // SPAN, SPAN, INNER)
    block_width = INNER // N_HEAD

    def project_rows(row_block):
        total = jnp.zeros((SPAN, D_MODEL), jnp.float32)
        for index in range(N_HEAD):
            part = jnp.dot(row_block[:, index * block_width:(index + 1) * block_width], out_weight[index * block_width:(index + 1) * block_width], preferred_element_type=jnp.float32).astype(jnp.bfloat16)
            part = lax.optimization_barrier(part)
            total = total + part.astype(jnp.float32)
        return total.astype(jnp.bfloat16)
    mixed = lax.map(project_rows, rows)
    return mixed.reshape(SEQS, LEN, D_MODEL)
```

```python
import functools

import jax
import jax.numpy as jnp
from jax import lax
from jax.experimental import pallas as pl
from jax.experimental.pallas import tpu as pltpu
from jax.sharding import PartitionSpec as P

HEAD_DIM = 64
STATE = 128
CONV = 4
SPAN = 128
RIM = 16
ROWS = 64
COLS = 256
F32 = jnp.float32
BF16 = jnp.bfloat16


def shifted(value, axis, steps):
    count = lax.axis_size(axis)
    initial, last = (max(0, -steps), min(count, count - steps))
    return lax.ppermute(value, axis, [(source, source + steps) for source in range(initial, last)])


def conv_into(out_ref, in_ref, rim_ref, taps_ref):
    length, width = in_ref.shape[1:]
    cols = min(COLS, width)
    for c in range(0, width, cols):
        taps = taps_ref[:, c : c + cols]
        for r in range(0, length, ROWS):
            if r == 0:
                tile = jnp.concatenate(
                    [rim_ref[0, :, c : c + cols], in_ref[0, 0:ROWS, c : c + cols]], axis=0
                )
            else:
                tile = in_ref[0, r - RIM : r + ROWS, c : c + cols]
            tile = tile.astype(F32)
            total = taps[CONV - 1 : CONV] * tile[RIM:]
            for tap in range(CONV - 1):
                start = RIM - (CONV - 1) + tap
                total = total + taps[tap : tap + 1] * tile[start : start + ROWS]
            total = total / (1.0 + jnp.exp(-total))
            out_ref[0, r : r + ROWS, c : c + cols] = total.astype(out_ref.dtype)


def local_kernel(
    x_ref, w_ref, r_ref, xr_ref, wr_ref, rr_ref, xt_ref, wt_ref, rt_ref, win_ref, exp_ref,
    v_out, w_out, r_out, s_out,
):
    conv_into(w_out, w_ref, wr_ref, wt_ref)
    conv_into(r_out, r_ref, rr_ref, rt_ref)
    conv_into(v_out, x_ref, xr_ref, xt_ref)
    length = v_out.shape[1]
    total = None
    for r in range(0, length, SPAN):
        spread = jnp.dot(win_ref[0, 0, r : r + SPAN, :], exp_ref[...], preferred_element_type=F32)
        scaled = (v_out[0, r : r + SPAN, :].astype(F32) * spread).astype(BF16)
        part = lax.dot_general(
            w_out[0, r : r + SPAN, :], scaled, (((0,), (0,)), ((), ())), preferred_element_type=F32
        )
        total = part if total is None else total + part
    s_out[0] = total.astype(s_out.dtype)


def scan_kernel(
    per_group, v_ref, w_ref, r_ref, gate_ref, ct_ref, cr_ref, st_ref, et_ref, wn_ref, dec_ref,
    carry_ref, gain_ref, exp_ref, out_ref, state_ref,
):
    @pl.when(pl.program_id(2) == 0)
    def _():
        state_ref[...] = carry_ref[0]

    writes, reads = w_ref[0], r_ref[0]
    scores = lax.dot_general(reads, writes, (((1,), (1,)), ((), ())), preferred_element_type=F32)
    rows = lax.broadcasted_iota(jnp.int32, (SPAN, SPAN), 0)
    cols = lax.broadcasted_iota(jnp.int32, (SPAN, SPAN), 1)
    later = rows >= cols
    scores = jnp.where(later, scores, 0.0)
    values = v_ref[0]
    spread = jnp.dot(et_ref[0, 0], exp_ref[...], preferred_element_type=F32)
    reading = jnp.dot(reads, state_ref[...].astype(BF16), preferred_element_type=F32) * spread
    half = lax.broadcasted_iota(jnp.int32, (SPAN, 2 * HEAD_DIM), 1) < HEAD_DIM
    squares = jnp.zeros((SPAN, 1), F32)
    parts = []
    for pair in range(per_group // 2):
        mixes = []
        for head in (2 * pair, 2 * pair + 1):
            gap = ct_ref[0, 0, :, head : head + 1] - cr_ref[0, 0, head : head + 1, :]
            gap = jnp.where(later, gap, 0.0)
            mixes.append((jnp.exp(gap) * st_ref[0, 0, head : head + 1, :] * scores).astype(BF16))
        at = slice(pair * 2 * HEAD_DIM, (pair + 1) * 2 * HEAD_DIM)
        both = values[:, at]
        zero = jnp.zeros_like(both)
        stacked = jnp.concatenate([jnp.where(half, both, zero), jnp.where(half, zero, both)], axis=0)
        ssd = jnp.dot(jnp.concatenate(mixes, axis=1), stacked, preferred_element_type=F32)
        ssd = ssd + reading[:, at]
        gate = gate_ref[0, :, at].astype(F32)
        gated = ssd * (gate / (1.0 + jnp.exp(-gate)))
        squares = squares + jnp.sum(gated * gated, axis=1, keepdims=True)
        parts.append(gated)
    scale = lax.rsqrt(squares / (per_group * HEAD_DIM) + 1e-05)
    for pair in range(per_group // 2):
        at = slice(pair * 2 * HEAD_DIM, (pair + 1) * 2 * HEAD_DIM)
        out_ref[0, :, at] = (parts[pair] * scale * gain_ref[:, at]).astype(BF16)

    @pl.when(pl.program_id(2) < pl.num_programs(2) - 1)
    def _():
        weight = jnp.dot(wn_ref[0, 0], exp_ref[...], preferred_element_type=F32)
        scaled = (values.astype(F32) * weight).astype(BF16)
        fresh = lax.dot_general(
            writes, scaled, (((0,), (0,)), ((), ())), preferred_element_type=F32
        )
        state_ref[...] = state_ref[...] * dec_ref[0, 0] + fresh


def project(normed, out_weight, n_head):
    seqs, length, _ = normed.shape
    gathered = lax.all_gather(out_weight, "seq", axis=0)
    pieces = gathered.shape[0] // n_head
    me = lax.axis_index("head")

    def partial(rows, block):
        block = jnp.clip(block, 0, n_head - 1)
        cut = lax.dynamic_slice_in_dim(gathered, block * pieces, pieces, 0)
        return jnp.concatenate(
            [jnp.dot(rows, cut[p], preferred_element_type=F32) for p in range(pieces)], axis=1
        )

    sums = [[None, None] for _ in range(seqs)]
    for slot in range(1, n_head):
        for s in range(seqs):
            for way, sign in ((0, 1), (1, -1)):
                term = partial(normed[s], me + sign * (n_head - slot))
                if sums[s][way] is not None:
                    term = term + sums[s][way].astype(F32)
                if sign > 0:
                    pairs = [(z, z + 1) for z in range(slot)]
                else:
                    pairs = [(n_head - 1 - z, n_head - 2 - z) for z in range(slot)]
                sums[s][way] = lax.ppermute(term.astype(BF16), "head", pairs)
    outs = [
        (partial(normed[s], me) + sums[s][0].astype(F32) + sums[s][1].astype(F32)).astype(BF16)
        for s in range(seqs)
    ]
    return jnp.stack(outs, axis=0)


def per_device(
    n_head,
    head_inputs,
    gate_inputs,
    state_writes,
    state_reads,
    step_raw,
    decay_log,
    conv_inputs,
    conv_writes,
    conv_reads,
    norm_gain,
    out_weight,
):
    seqs, length, width = head_inputs.shape
    heads = decay_log.shape[0]
    groups = state_writes.shape[2] // STATE
    per_group = heads // groups
    gw = width // groups
    spans = length // SPAN
    rims = shifted(
        (
            head_inputs[:, length - RIM :],
            state_writes[:, length - RIM :],
            state_reads[:, length - RIM :],
        ),
        "seq",
        1,
    )
    steps = jax.nn.softplus(step_raw)
    log_decay = steps * (-jnp.exp(decay_log))[None, :, None]
    steps_blocks = steps.reshape(seqs, heads, spans, SPAN)
    cumul = jnp.cumsum(log_decay.reshape(seqs, heads, spans, SPAN), axis=-1)
    ends = cumul[..., -1]
    after = jnp.flip(jnp.cumsum(jnp.flip(ends, -1), -1), -1) - ends

    def by_time(x):
        x = x.reshape(seqs, groups, per_group, length)
        return x.transpose(0, 1, 3, 2)

    def by_head(x):
        x = x.reshape(seqs, groups, per_group, spans, SPAN).transpose(0, 1, 3, 2, 4)
        return x.reshape(seqs, groups * spans, per_group, SPAN)

    ct = by_time(cumul)
    et = by_time(jnp.exp(cumul)).astype(BF16)
    win = jnp.exp(ends[..., None] - cumul) * steps_blocks
    wn = by_time(win).astype(BF16)
    wfar = by_time(jnp.exp(after[..., None] + ends[..., None] - cumul) * steps_blocks).astype(BF16)
    cr, st = by_head(cumul), by_head(steps_blocks)
    dec = jnp.repeat(jnp.exp(ends).transpose(0, 2, 1), HEAD_DIM, axis=2)[:, :, None, :]
    expand = (jnp.arange(per_group)[:, None] == jnp.arange(gw)[None, :] // HEAD_DIM).astype(BF16)

    def spec(shape, index):
        return pl.BlockSpec(shape, index)

    tall = lambda w: spec((1, length, w), lambda s, g: (s, 0, g))
    edge = lambda w: spec((1, RIM, w), lambda s, g: (s, 0, g))
    tap = lambda w: spec((CONV, w), lambda s, g: (0, g))
    values, writes, reads, finals = pl.pallas_call(
        local_kernel,
        grid=(seqs, groups),
        in_specs=[
            tall(gw), tall(STATE), tall(STATE), edge(gw), edge(STATE), edge(STATE),
            tap(gw), tap(STATE), tap(STATE),
            spec((1, 1, length, per_group), lambda s, g: (s, g, 0, 0)),
            spec((per_group, gw), lambda s, g: (0, 0)),
        ],
        out_specs=[
            tall(gw), tall(STATE), tall(STATE),
            spec((1, STATE, gw), lambda s, g: (s, 0, g)),
        ],
        out_shape=[
            jax.ShapeDtypeStruct((seqs, length, width), BF16),
            jax.ShapeDtypeStruct((seqs, length, groups * STATE), BF16),
            jax.ShapeDtypeStruct((seqs, length, groups * STATE), BF16),
            jax.ShapeDtypeStruct((seqs, STATE, width), BF16),
        ],
        compiler_params=pltpu.CompilerParams(vmem_limit_bytes=48 * 2**20),
        cost_estimate=pl.CostEstimate(
            flops=4 * seqs * length * STATE * width,
            bytes_accessed=4 * seqs * length * width,
            transcendentals=seqs * length * width,
        ),
        name="local_states",
    )(head_inputs, state_writes, state_reads, *rims, conv_inputs, conv_writes, conv_reads, wfar, expand)

    device_logs = jnp.sum(ends, axis=-1)
    all_logs = lax.all_gather(device_logs[None], "seq", axis=0, tiled=True)
    before = jnp.cumsum(all_logs, axis=0) - all_logs
    own = lax.axis_index("seq")
    own_before = lax.dynamic_index_in_dim(before, own, 0, keepdims=False)
    pieces = lax.all_gather(finals, "seq", axis=0)
    source = jnp.arange(pieces.shape[0], dtype=jnp.int32)
    far = jnp.where((source < own)[:, None, None], own_before[None] - before - all_logs, -jnp.inf)
    far = jnp.repeat(jnp.exp(far), HEAD_DIM, axis=2)
    carried = jnp.sum(far[:, :, None, :] * pieces.astype(F32), axis=0)

    block = lambda w: spec((1, SPAN, w), lambda s, g, c: (s, c, g))
    timed = spec((1, 1, SPAN, per_group), lambda s, g, c: (s, g, c, 0))
    headed = spec((1, 1, per_group, SPAN), lambda s, g, c: (s, g * spans + c, 0, 0))
    normed = pl.pallas_call(
        functools.partial(scan_kernel, per_group),
        grid=(seqs, groups, spans),
        in_specs=[
            block(gw), block(STATE), block(STATE), block(gw),
            timed, headed, headed, timed, timed,
            spec((1, 1, 1, gw), lambda s, g, c: (s, c, 0, g)),
            spec((1, STATE, gw), lambda s, g, c: (s, 0, g)),
            spec((1, gw), lambda s, g, c: (0, g)),
            spec((per_group, gw), lambda s, g, c: (0, 0)),
        ],
        out_specs=block(gw),
        out_shape=jax.ShapeDtypeStruct((seqs, length, width), BF16),
        scratch_shapes=[pltpu.VMEM((STATE, gw), F32)],
        compiler_params=pltpu.CompilerParams(vmem_limit_bytes=48 * 2**20),
        cost_estimate=pl.CostEstimate(
            flops=8 * seqs * length * STATE * width,
            bytes_accessed=6 * seqs * length * width,
            transcendentals=4 * seqs * length * width,
        ),
        name="span_scan",
    )(values, writes, reads, gate_inputs, ct, cr, st, et, wn, dec, carried, norm_gain[None], expand)
    return project(normed, out_weight, n_head)


def solution(mesh):
    return jax.shard_map(
        functools.partial(per_device, mesh.shape["head"]),
        mesh=mesh,
        in_specs=(
            P(None, "seq", "head"),
            P(None, "seq", "head"),
            P(None, "seq", "head"),
            P(None, "seq", "head"),
            P(None, "head", "seq"),
            P("head"),
            P(None, "head"),
            P(None, "head"),
            P(None, "head"),
            P("head"),
            P("head", "seq"),
        ),
        out_specs=P(None, "seq", "head"),
        check_vma=False,
    )
```

```python
import functools

import jax
import jax.numpy as jnp
from jax import lax
from jax.experimental import pallas as pl
from jax.experimental.pallas import tpu as pltpu
from jax.sharding import PartitionSpec as P

HEAD_DIM = 64
STATE = 128
CONV = 4
SPAN = 128
RIM = 16
ROWS = 64
COLS = 256
F32 = jnp.float32
BF16 = jnp.bfloat16


def shifted(value, axis, steps):
    count = lax.axis_size(axis)
    initial, last = (max(0, -steps), min(count, count - steps))
    return lax.ppermute(value, axis, [(source, source + steps) for source in range(initial, last)])


def conv_into(out_ref, in_ref, rim_ref, taps_ref):
    length, width = in_ref.shape[1:]
    cols = min(COLS, width)
    for c in range(0, width, cols):
        taps = taps_ref[:, c : c + cols]
        for r in range(0, length, ROWS):
            if r == 0:
                tile = jnp.concatenate(
                    [rim_ref[0, :, c : c + cols], in_ref[0, 0:ROWS, c : c + cols]], axis=0
                )
            else:
                tile = in_ref[0, r - RIM : r + ROWS, c : c + cols]
            tile = tile.astype(F32)
            total = taps[CONV - 1 : CONV] * tile[RIM:]
            for tap in range(CONV - 1):
                start = RIM - (CONV - 1) + tap
                total = total + taps[tap : tap + 1] * tile[start : start + ROWS]
            total = total / (1.0 + jnp.exp(-total))
            out_ref[0, r : r + ROWS, c : c + cols] = total.astype(out_ref.dtype)


def local_kernel(
    x_ref, w_ref, r_ref, xr_ref, wr_ref, rr_ref, xt_ref, wt_ref, rt_ref, win_ref, exp_ref,
    v_out, w_out, r_out, s_out,
):
    conv_into(w_out, w_ref, wr_ref, wt_ref)
    conv_into(r_out, r_ref, rr_ref, rt_ref)
    conv_into(v_out, x_ref, xr_ref, xt_ref)
    length = v_out.shape[1]
    total = None
    for r in range(0, length, SPAN):
        spread = jnp.dot(win_ref[0, 0, r : r + SPAN, :], exp_ref[...], preferred_element_type=F32)
        scaled = (v_out[0, r : r + SPAN, :].astype(F32) * spread).astype(BF16)
        part = lax.dot_general(
            w_out[0, r : r + SPAN, :], scaled, (((0,), (0,)), ((), ())), preferred_element_type=F32
        )
        total = part if total is None else total + part
    s_out[0] = total.astype(s_out.dtype)


def scan_kernel(
    per_group, v_ref, w_ref, r_ref, gate_ref, ct_ref, cr_ref, st_ref, et_ref, wn_ref, dec_ref,
    carry_ref, gain_ref, exp_ref, out_ref, state_ref,
):
    @pl.when(pl.program_id(2) == 0)
    def _():
        state_ref[...] = carry_ref[0]

    writes, reads = w_ref[0], r_ref[0]
    scores = lax.dot_general(reads, writes, (((1,), (1,)), ((), ())), preferred_element_type=F32)
    rows = lax.broadcasted_iota(jnp.int32, (SPAN, SPAN), 0)
    cols = lax.broadcasted_iota(jnp.int32, (SPAN, SPAN), 1)
    later = rows >= cols
    scores = jnp.where(later, scores, 0.0)
    values = v_ref[0]
    spread = jnp.dot(et_ref[0, 0], exp_ref[...], preferred_element_type=F32)
    reading = jnp.dot(reads, state_ref[...].astype(BF16), preferred_element_type=F32) * spread
    half = lax.broadcasted_iota(jnp.int32, (SPAN, 2 * HEAD_DIM), 1) < HEAD_DIM
    squares = jnp.zeros((SPAN, 1), F32)
    parts = []
    for pair in range(per_group // 2):
        mixes = []
        for head in (2 * pair, 2 * pair + 1):
            gap = ct_ref[0, 0, :, head : head + 1] - cr_ref[0, 0, head : head + 1, :]
            gap = jnp.where(later, gap, 0.0)
            mixes.append((jnp.exp(gap) * st_ref[0, 0, head : head + 1, :] * scores).astype(BF16))
        at = slice(pair * 2 * HEAD_DIM, (pair + 1) * 2 * HEAD_DIM)
        both = values[:, at]
        zero = jnp.zeros_like(both)
        stacked = jnp.concatenate([jnp.where(half, both, zero), jnp.where(half, zero, both)], axis=0)
        ssd = jnp.dot(jnp.concatenate(mixes, axis=1), stacked, preferred_element_type=F32)
        ssd = ssd + reading[:, at]
        gate = gate_ref[0, :, at].astype(F32)
        gated = ssd * (gate / (1.0 + jnp.exp(-gate)))
        squares = squares + jnp.sum(gated * gated, axis=1, keepdims=True)
        parts.append(gated)
    scale = lax.rsqrt(squares / (per_group * HEAD_DIM) + 1e-05)
    for pair in range(per_group // 2):
        at = slice(pair * 2 * HEAD_DIM, (pair + 1) * 2 * HEAD_DIM)
        out_ref[0, :, at] = (parts[pair] * scale * gain_ref[:, at]).astype(BF16)

    @pl.when(pl.program_id(2) < pl.num_programs(2) - 1)
    def _():
        weight = jnp.dot(wn_ref[0, 0], exp_ref[...], preferred_element_type=F32)
        scaled = (values.astype(F32) * weight).astype(BF16)
        fresh = lax.dot_general(
            writes, scaled, (((0,), (0,)), ((), ())), preferred_element_type=F32
        )
        state_ref[...] = state_ref[...] * dec_ref[0, 0] + fresh


def chain_kernel(n, chunk, a_ref, w_ref, out_ref, buf, send_sem, recv_sem):
    me = lax.axis_index("head")
    rows = a_ref.shape[0]
    pieces, cols = w_ref.shape[0] // n, w_ref.shape[2]
    chunks = rows // chunk
    ways = ((0, 1), (1, -1))
    depths = (me, n - 1 - me)
    nexts = (lax.rem(me + 1, n), lax.rem(me + n - 1, n))

    def copy(way, slot, q):
        at = pl.ds(pl.multiple_of(q * chunk, chunk), chunk)
        return pltpu.make_async_remote_copy(
            src_ref=buf.at[way, slot - 1, at],
            dst_ref=buf.at[way, slot, at],
            send_sem=send_sem.at[way, slot - 1, q],
            recv_sem=recv_sem.at[way, slot - 1, q],
            device_id={"head": nexts[way]},
            device_id_type=pl.DeviceIdType.MESH,
        )

    barrier = pltpu.get_barrier_semaphore()
    for way, _ in ways:

        @pl.when(depths[way] < n - 1)
        def _():
            pl.semaphore_signal(
                barrier,
                inc=1,
                device_id={"head": nexts[way]},
                device_id_type=pl.DeviceIdType.MESH,
            )

    outer = jnp.logical_or(me == 0, me == n - 1)

    @pl.when(outer)
    def _():
        pl.semaphore_wait(barrier, 1)

    @pl.when(jnp.logical_not(outer))
    def _():
        pl.semaphore_wait(barrier, 2)

    def send(index, carry):
        slot, q = index // chunks + 1, index % chunks
        at = pl.ds(pl.multiple_of(q * chunk, chunk), chunk)
        for way, sign in ways:

            @pl.when(depths[way] < slot)
            def _():
                block = me + sign * (n - slot)

                @pl.when(depths[way] == 0)
                def _():
                    buf[way, slot - 1, at, :] = jnp.zeros((chunk, pieces * cols), BF16)

                @pl.when(depths[way] > 0)
                def _():
                    copy(way, slot - 1, q).wait_recv()

                for p in range(pieces):
                    term = jnp.dot(a_ref[at, :], w_ref[block * pieces + p], preferred_element_type=F32)
                    lanes = slice(p * cols, (p + 1) * cols)
                    term = term + buf[way, slot - 1, at, lanes].astype(F32)
                    buf[way, slot - 1, at, lanes] = term.astype(BF16)
                copy(way, slot, q).start()

        return carry

    lax.fori_loop(0, (n - 1) * chunks, send, 0)

    def finish(q, carry):
        at = pl.ds(pl.multiple_of(q * chunk, chunk), chunk)
        for way, _ in ways:

            @pl.when(depths[way] == 0)
            def _():
                buf[way, n - 1, at, :] = jnp.zeros((chunk, pieces * cols), BF16)

            @pl.when(depths[way] > 0)
            def _():
                copy(way, n - 1, q).wait_recv()

        for p in range(pieces):
            lanes = slice(p * cols, (p + 1) * cols)
            term = jnp.dot(a_ref[at, :], w_ref[me * pieces + p], preferred_element_type=F32)
            term = term + buf[0, n - 1, at, lanes].astype(F32) + buf[1, n - 1, at, lanes].astype(F32)
            out_ref[at, lanes] = term.astype(BF16)
        return carry

    lax.fori_loop(0, chunks, finish, 0)

    def drain(index, carry):
        slot, q = index // chunks + 1, index % chunks
        for way, _ in ways:

            @pl.when(depths[way] < slot)
            def _():
                copy(way, slot, q).wait_send()

        return carry

    lax.fori_loop(0, (n - 1) * chunks, drain, 0)


def chain_sum(rows, gathered, n_head, chunk, part):
    count, depth, cols = gathered.shape
    width = count // n_head * cols
    total = rows.shape[0]
    return pl.pallas_call(
        functools.partial(chain_kernel, n_head, chunk),
        out_shape=jax.ShapeDtypeStruct((total, width), BF16),
        in_specs=[pl.BlockSpec(memory_space=pltpu.VMEM)] * 2,
        out_specs=pl.BlockSpec(memory_space=pltpu.VMEM),
        scratch_shapes=[
            pltpu.VMEM((2, n_head, total, width), BF16),
            pltpu.SemaphoreType.DMA((2, n_head - 1, total // chunk)),
            pltpu.SemaphoreType.DMA((2, n_head - 1, total // chunk)),
        ],
        compiler_params=pltpu.CompilerParams(
            collective_id=part, has_side_effects=True, vmem_limit_bytes=56 * 2**20
        ),
        cost_estimate=pl.CostEstimate(
            flops=16 * total * depth * count * cols,
            bytes_accessed=2 * count * depth * cols,
            transcendentals=0,
        ),
        name="chain_sum",
    )(rows, gathered)


def paired(value, bit):
    count = lax.axis_size("seq")
    return lax.ppermute(value, "seq", [(s, s ^ bit) for s in range(count)])


def carry_in(finals, before, totals):
    count = before.shape[0]
    own = lax.axis_index("seq")
    width = finals.shape[2]
    half = width // 2
    before = jnp.concatenate([before, before[-1:] + totals[-1:]], axis=0)

    def at(index):
        return lax.dynamic_index_in_dim(before, index, 0, keepdims=False)

    def decay(start, end):
        return jnp.repeat(jnp.exp(at(end) - at(start)), HEAD_DIM, axis=1)[:, None, :]

    odd = own % 2
    mine = lambda x: lax.dynamic_slice_in_dim(x, odd * half, half, 2)
    other = paired(finals, 1)
    own_h, other_h = mine(finals).astype(F32), mine(other).astype(F32)
    first = jnp.where(odd == 1, other_h, own_h)
    second = jnp.where(odd == 1, own_h, other_h)
    pair = own - odd
    total = mine(decay(pair + 1, pair + 2)) * first + second
    prefix = jnp.zeros_like(total)
    bit = 2
    while bit < count:
        got = paired(total.astype(BF16), bit).astype(F32)
        upper = (own // bit) % 2 == 1
        base = own // bit * bit
        low = jnp.where(upper, base - bit, base)
        prefix = jnp.where(upper, mine(decay(base, pair)) * got + prefix, prefix)
        first = jnp.where(upper, got, total)
        second = jnp.where(upper, total, got)
        total = mine(decay(low + bit, low + 2 * bit)) * first + second
        bit *= 2
    held = prefix.astype(BF16)
    swapped = paired(held, 1)
    left = jnp.where(odd == 1, swapped, held)
    right = jnp.where(odd == 1, held, swapped)
    whole = jnp.concatenate([left, right], axis=2).astype(F32)
    return jnp.where(odd == 1, decay(pair, pair + 1) * whole + other.astype(F32), whole)


def per_device(
    n_head,
    head_inputs,
    gate_inputs,
    state_writes,
    state_reads,
    step_raw,
    decay_log,
    conv_inputs,
    conv_writes,
    conv_reads,
    norm_gain,
    out_weight,
):
    seqs, length, width = head_inputs.shape
    heads = decay_log.shape[0]
    groups = state_writes.shape[2] // STATE
    per_group = heads // groups
    gw = width // groups
    spans = length // SPAN
    rims = shifted(
        (
            head_inputs[:, length - RIM :],
            state_writes[:, length - RIM :],
            state_reads[:, length - RIM :],
        ),
        "seq",
        1,
    )
    steps = jax.nn.softplus(step_raw)
    log_decay = steps * (-jnp.exp(decay_log))[None, :, None]
    steps_blocks = steps.reshape(seqs, heads, spans, SPAN)
    cumul = jnp.cumsum(log_decay.reshape(seqs, heads, spans, SPAN), axis=-1)
    ends = cumul[..., -1]
    after = jnp.flip(jnp.cumsum(jnp.flip(ends, -1), -1), -1) - ends

    def by_time(x):
        x = x.reshape(seqs, groups, per_group, length)
        return x.transpose(0, 1, 3, 2)

    def by_head(x):
        x = x.reshape(seqs, groups, per_group, spans, SPAN).transpose(0, 1, 3, 2, 4)
        return x.reshape(seqs, groups * spans, per_group, SPAN)

    ct = by_time(cumul)
    et = by_time(jnp.exp(cumul)).astype(BF16)
    win = jnp.exp(ends[..., None] - cumul) * steps_blocks
    wn = by_time(win).astype(BF16)
    wfar = by_time(jnp.exp(after[..., None] + ends[..., None] - cumul) * steps_blocks).astype(BF16)
    cr, st = by_head(cumul), by_head(steps_blocks)
    dec = jnp.repeat(jnp.exp(ends).transpose(0, 2, 1), HEAD_DIM, axis=2)[:, :, None, :]
    expand = (jnp.arange(per_group)[:, None] == jnp.arange(gw)[None, :] // HEAD_DIM).astype(BF16)

    def spec(shape, index):
        return pl.BlockSpec(shape, index)

    tall = lambda w: spec((1, length, w), lambda s, g: (s, 0, g))
    edge = lambda w: spec((1, RIM, w), lambda s, g: (s, 0, g))
    tap = lambda w: spec((CONV, w), lambda s, g: (0, g))
    values, writes, reads, finals = pl.pallas_call(
        local_kernel,
        grid=(seqs, groups),
        in_specs=[
            tall(gw), tall(STATE), tall(STATE), edge(gw), edge(STATE), edge(STATE),
            tap(gw), tap(STATE), tap(STATE),
            spec((1, 1, length, per_group), lambda s, g: (s, g, 0, 0)),
            spec((per_group, gw), lambda s, g: (0, 0)),
        ],
        out_specs=[
            tall(gw), tall(STATE), tall(STATE),
            spec((1, STATE, gw), lambda s, g: (s, 0, g)),
        ],
        out_shape=[
            jax.ShapeDtypeStruct((seqs, length, width), BF16),
            jax.ShapeDtypeStruct((seqs, length, groups * STATE), BF16),
            jax.ShapeDtypeStruct((seqs, length, groups * STATE), BF16),
            jax.ShapeDtypeStruct((seqs, STATE, width), BF16),
        ],
        compiler_params=pltpu.CompilerParams(vmem_limit_bytes=48 * 2**20),
        cost_estimate=pl.CostEstimate(
            flops=4 * seqs * length * STATE * width,
            bytes_accessed=4 * seqs * length * width,
            transcendentals=seqs * length * width,
        ),
        name="local_states",
    )(head_inputs, state_writes, state_reads, *rims, conv_inputs, conv_writes, conv_reads, wfar, expand)

    device_logs = jnp.sum(ends, axis=-1)
    all_logs = lax.all_gather(device_logs[None], "seq", axis=0, tiled=True)
    before = jnp.cumsum(all_logs, axis=0) - all_logs
    carried = carry_in(finals, before, all_logs)
    cols = out_weight.shape[1] // 2
    early = lax.all_gather(out_weight[:, :cols], "seq", axis=0)
    late = lax.all_gather(out_weight[:, cols:], "seq", axis=0)
    carried, early = lax.optimization_barrier((carried, early))

    block = lambda w: spec((1, SPAN, w), lambda s, g, c: (s, c, g))
    timed = spec((1, 1, SPAN, per_group), lambda s, g, c: (s, g, c, 0))
    headed = spec((1, 1, per_group, SPAN), lambda s, g, c: (s, g * spans + c, 0, 0))
    normed = pl.pallas_call(
        functools.partial(scan_kernel, per_group),
        grid=(seqs, groups, spans),
        in_specs=[
            block(gw), block(STATE), block(STATE), block(gw),
            timed, headed, headed, timed, timed,
            spec((1, 1, 1, gw), lambda s, g, c: (s, c, 0, g)),
            spec((1, STATE, gw), lambda s, g, c: (s, 0, g)),
            spec((1, gw), lambda s, g, c: (0, g)),
            spec((per_group, gw), lambda s, g, c: (0, 0)),
        ],
        out_specs=block(gw),
        out_shape=jax.ShapeDtypeStruct((seqs, length, width), BF16),
        scratch_shapes=[pltpu.VMEM((STATE, gw), F32)],
        compiler_params=pltpu.CompilerParams(vmem_limit_bytes=48 * 2**20),
        cost_estimate=pl.CostEstimate(
            flops=8 * seqs * length * STATE * width,
            bytes_accessed=6 * seqs * length * width,
            transcendentals=4 * seqs * length * width,
        ),
        name="span_scan",
    )(values, writes, reads, gate_inputs, ct, cr, st, et, wn, dec, carried, norm_gain[None], expand)
    rows = normed.reshape(seqs * length, width)
    chunk = rows.shape[0] // 4
    sums = [chain_sum(rows, early, n_head, chunk, 0)]
    rows, sums[0] = lax.optimization_barrier((rows, sums[0]))
    sums.append(chain_sum(rows, late, n_head, chunk, 1))
    sums = [x.reshape(seqs, length, -1, cols) for x in sums]
    return jnp.concatenate(sums, axis=3).reshape(seqs, length, -1)


def solution(mesh):
    return jax.shard_map(
        functools.partial(per_device, mesh.shape["head"]),
        mesh=mesh,
        in_specs=(
            P(None, "seq", "head"),
            P(None, "seq", "head"),
            P(None, "seq", "head"),
            P(None, "seq", "head"),
            P(None, "head", "seq"),
            P("head"),
            P(None, "head"),
            P(None, "head"),
            P(None, "head"),
            P("head"),
            P("head", "seq"),
        ),
        out_specs=P(None, "seq", "head"),
        check_vma=False,
    )
```
